32 devices in a mesh: dp: 2 (over x), ctx: 16 (over z, y, core).
Axes of the slice: x: 2, y: 2, z: 4, core: 2. Of those that a mesh axis runs over, the one named last changes fastest.
Arguments:
- gate_branch: bfloat16 [4096, 4096], P(('dp', 'ctx')), may hold values from -6 to 6
- conv_input: bfloat16 [4096, 4096], P(('dp', 'ctx')), may hold values from -6 to 6
- grad_output: bfloat16 [4096, 4096], P(('dp', 'ctx')), may hold values from -6 to 6
- filter_taps: float32 [256, 128], replicated, may hold values from -0.5 to 0.5
- document_lengths: int32 [2, 16], P('dp'), may hold values from 1 to 512, 2048 in all within a row
Outputs:
- grad_input: bfloat16 [4096, 4096], P(('dp', 'ctx'))
- filter_grad: float32 [256, 128], P('ctx')
The draws below stay inside these ranges and needn't reach their ends.
Inputs may be any that keep to these rules, and one draw needn't show every extreme that they name: `document_lengths`: each row holds the lengths of 16 documents packed end to end in one data group's 2048 tokens; they sum to 2048.
All inputs are finite; a program needn't handle non-finite values.
Results may differ from the reference program's by a relative error of at most 0.0057.
Values may be sent and summed in bfloat16 or wider, within the bound.
No kernel may reach another device: no remote copies, remote signals or barrier semaphores. Data moves between devices by JAX's collectives and lax.ppermute only.
A program may use at most 128 MiB of HBM per device.

```python
import math
import jax
import jax.numpy as jnp
import numpy as np
from jax import lax

D = 4096
FILT = 128
GROUP = 16
DOCS = 16
TOKENS = 2048
ROWS = 4096
GROUPS = 256
MOST = 512
N_DP = 2


def with_spikes(result, own_key, source, target, parts, factor):
    owner, partner = [(jnp.arange(result.shape[axis_at]) // (result.shape[axis_at] // parts)).reshape([-1 if axis == axis_at else 1 for axis in range(result.ndim)]) for axis_at in (source, target)]
    chosen = jax.random.permutation(own_key, parts)[partner]
    strong = (owner == chosen) | (owner == (partner + parts // 2) % parts)
    return jnp.where(strong, factor * result, result)


def levels(stream_key, dims, split, smallest, top_value):
    level, own = 1.0, jax.random.fold_in(stream_key, 6)
    for axis_at, shards_of in split:
        draws = jnp.exp(jax.random.uniform(jax.random.fold_in(own, axis_at), (shards_of,), jnp.float32, smallest / len(split), top_value / len(split)))
        level = level * jnp.repeat(draws, dims[axis_at] // shards_of).reshape([-1 if axis == axis_at else 1 for axis in range(len(dims))])
    return level


def length_profile(amount, total, most, lean):
    loads = [(1 << 20) // math.isqrt(grade ** lean) + 1 for grade in range(2, amount + 1)]
    surplus, given = total - most - (amount - 1), [1] * (amount - 1)
    while surplus > 0:
        free = [i for i in range(amount - 1) if given[i] < most]
        pool, budget = sum([loads[i] for i in free]), surplus
        for i in free:
            extra = min(most - given[i], max(1, budget * loads[i] // pool), surplus)
            given[i] = given[i] + extra
            surplus = surplus - extra
    return np.array([most] + given)


def uneven_parts(key, number_of, total, limit, skew):
    if number_of == 2:
        one = jax.random.randint(key, (), max(1, total - limit), min(limit, total - 1) + 1)
        return jnp.stack([one, total - one])
    sizes = jnp.asarray(length_profile(number_of, total, limit, skew), jnp.int32)
    couples = (number_of - 1) // 2
    donor, receiver = sizes[1:1 + 2 * couples:2], sizes[2:2 + 2 * couples:2]
    slack = jnp.minimum(donor - 1, limit - receiver)
    passed = jax.random.randint(jax.random.fold_in(key, 1), (couples,), 0, 1 << 20) % (slack + 1)
    sizes = sizes.at[1:1 + 2 * couples:2].set(donor - passed).at[2:2 + 2 * couples:2].set(receiver + passed)
    return sizes[jax.random.permutation(jax.random.fold_in(key, 2), number_of)]


def scatter_about(stream_key, shape, scale, bound, cuts=(), kind=jnp.bfloat16):
    entries = scale * jax.random.normal(stream_key, shape, jnp.float32)
    if cuts:
        entries = entries * levels(stream_key, shape, cuts, -0.22, 0.18)
    return jnp.clip(entries, -bound, bound).astype(kind)


def gaussian_with(stream_key, extent, deviation, most, cuts, heavy, held_as=jnp.bfloat16):
    drawn = deviation * jax.random.normal(stream_key, extent, jnp.float32)
    if cuts:
        drawn = drawn * levels(stream_key, extent, cuts, -0.22, 0.18)
    return jnp.clip(with_spikes(drawn, jax.random.fold_in(stream_key, 3), *heavy), -most, most).astype(held_as)


def setup_inputs(seed: int = 0) -> dict:
    key_list = jax.random.split(jax.random.key(seed), 6)
    gate_branch = scatter_about(key_list[0], (ROWS, D), 1.0, 6.0, ((0, 32),))
    conv_input = scatter_about(key_list[1], (ROWS, D), 1.0, 6.0, ((0, 32),))
    grad_output = gaussian_with(key_list[2], (ROWS, D), 1.0, 6.0, ((0, 32),), (0, 1, 32, 2.75))
    filter_taps = scatter_about(key_list[3], (GROUPS, FILT), FILT ** -0.5, 0.5, (), jnp.float32)
    document_lengths = jax.vmap(lambda own: uneven_parts(own, DOCS, TOKENS, MOST, 2))(jax.random.split(key_list[4], N_DP)).reshape((N_DP, DOCS)).astype(jnp.int32)
    return dict(gate_branch=gate_branch, conv_input=conv_input, grad_output=grad_output, filter_taps=filter_taps, document_lengths=document_lengths)


def band_matrix(taps_half):
    tile_count = taps_half.shape[0]
    padded = jnp.concatenate([taps_half, jnp.zeros((tile_count, 129), taps_half.dtype)], axis=1)
    repeated = jnp.broadcast_to(padded[:, None, :], (tile_count, 128, 257)).reshape(tile_count, 128 * 257)
    return repeated[:, :128 * 256].reshape(tile_count, 128, 256)


def lag_sums(product):
    tile_count = product.shape[0]
    flattened = product.reshape(tile_count, 128 * 256)
    flattened = jnp.concatenate([flattened, jnp.zeros((tile_count, 128), product.dtype)], axis=1)
    skewed = flattened.reshape(tile_count, 128, 257)
    column = jnp.sum(skewed, axis=1)
    return column[:, 1:129][:, ::-1]


def segment_ids(places, document_ends):
    return jnp.sum((places[..., None] >= document_ends).astype(jnp.int32), axis=-1)


def block_grads(mixed_here, mixed_after, input_before, input_here, labels_before, labels_here, labels_after, taps_half):
    blocks = mixed_here.shape[0]
    channels = mixed_here.shape[2]
    groups = channels // GROUP
    group_tile = min(groups, 32)
    block_tile = math.gcd(blocks, max(1, 32 // group_tile))
    group_steps = groups // group_tile
    block_steps = blocks // block_tile
    band = band_matrix(taps_half).reshape(group_steps, group_tile, 128, 256)
    mixed_ext = jnp.concatenate([mixed_here, mixed_after], axis=1)
    input_ext = jnp.concatenate([input_before, input_here], axis=1)
    keep_down = labels_here[:, :, None] == jnp.concatenate([labels_here, labels_after], axis=1)[:, None, :]
    keep_lag = labels_here[:, :, None] == jnp.concatenate([labels_before, labels_here], axis=1)[:, None, :]
    keep_down = keep_down.reshape(block_steps, block_tile, 128, 256)
    keep_lag = keep_lag.reshape(block_steps, block_tile, 128, 256)

    def to_tiles(array_in):
        return jnp.moveaxis(array_in.reshape(block_steps, block_tile, 256, group_steps, group_tile, GROUP), 3, 0)

    mixed_tiles = to_tiles(mixed_ext)
    input_tiles = to_tiles(input_ext)

    def per_group(operands):
        band_tile, mixed_part, input_part = operands

        def per_block(pieces):
            mask_down, mask_lag, mixed_block, input_block = pieces
            kernel = band_tile[None] * mask_down[:, None].astype(jnp.bfloat16)
            down_part = jnp.einsum('bgij,bjgc->bigc', kernel.astype(jnp.float32), mixed_block.astype(jnp.float32))
            product = jnp.einsum('bigc,bjgc->bgij', mixed_block[:, :128].astype(jnp.float32), input_block.astype(jnp.float32))
            product = jnp.sum(jnp.where(mask_lag[:, None], product, jnp.float32(0.0)), axis=0)
            return down_part, lag_sums(product)

        return lax.map(per_block, (keep_down, keep_lag, mixed_part, input_part))

    down_all, lagged = lax.map(per_group, (band, mixed_tiles, input_tiles))
    down_all = jnp.moveaxis(down_all, 0, 3).reshape(blocks, 128, channels).astype(jnp.bfloat16)
    lagged = jnp.sum(lagged, axis=1).reshape(groups, 128)
    return down_all, lagged


def reference(gate_branch, conv_input, grad_output, filter_taps, document_lengths):
    taps_half = filter_taps.astype(jnp.bfloat16)
    blocks = TOKENS // 128

    def one_group(operands):
        gate_part, input_part, grad_part, lengths = operands
        mixed_grad = (grad_part.astype(jnp.float32) * gate_part.astype(jnp.float32)).astype(jnp.bfloat16)
        document_ends = jnp.cumsum(lengths).astype(jnp.int32)
        zero_block = jnp.zeros((1, 128, D), jnp.bfloat16)
        mixed_after = jnp.concatenate([mixed_grad[1:], zero_block], axis=0)
        input_before = jnp.concatenate([zero_block, input_part[:-1]], axis=0)
        places = jnp.arange(TOKENS, dtype=jnp.int32).reshape(blocks, 128)
        labels_here = segment_ids(places, document_ends)
        labels_before = segment_ids(places - 128, document_ends)
        labels_after = segment_ids(places + 128, document_ends)
        return block_grads(mixed_grad, mixed_after, input_before, input_part, labels_before, labels_here, labels_after, taps_half)

    down_all, lagged = lax.map(one_group, (gate_branch.reshape(N_DP, blocks, 128, D), conv_input.reshape(N_DP, blocks, 128, D), grad_output.reshape(N_DP, blocks, 128, D), document_lengths))
    grad_scale = (1.0 * GROUP * N_DP * TOKENS) ** -0.5
    grad_input = down_all.reshape(N_DP * TOKENS, D)
    filter_grad = jnp.sum(lagged, axis=0) * grad_scale
    return grad_input, filter_grad
```

```python
import functools

import jax
import jax.numpy as jnp
from jax import lax
from jax.experimental import pallas as pl
from jax.experimental.pallas import tpu as pltpu
from jax.sharding import PartitionSpec as P

GROUP = 16
FILT = 128
TILE = 256
HALF = 128
PAIRS = HALF // GROUP
BIG = 1 << 30
F32 = jnp.float32
BF16 = jnp.bfloat16


def document_masks(lens_ref, base, backwards):
    row = lax.broadcasted_iota(jnp.int32, (FILT, HALF), 0)
    if backwards:
        row = FILT - 1 - row
    column = lax.broadcasted_iota(jnp.int32, (FILT, HALF), 1)
    end_of = jnp.full((FILT, HALF), BIG, jnp.int32)
    end = -base
    for k in range(lens_ref.shape[1]):
        end = end + lens_ref[0, k]
        end_of = jnp.minimum(end_of, jnp.where(row < end, end, BIG))
    own = (column >= row) & (column < end_of)
    cross = (column < row) & (column + FILT < end_of)
    return own, cross


def lane_group():
    lane = lax.broadcasted_iota(jnp.int32, (FILT, TILE), 1)
    return (lane % HALF) // GROUP


def two_halves(rows):
    lane = lax.broadcasted_iota(jnp.int32, (FILT, TILE), 1)
    zero = jnp.zeros_like(rows)
    return jnp.concatenate([jnp.where(lane < HALF, rows, zero), jnp.where(lane >= HALF, rows, zero)], axis=0)


def split_groups(rows):
    which = lane_group()
    zero = jnp.zeros_like(rows)
    return jnp.concatenate([jnp.where(which == p, rows, zero) for p in range(PAIRS)], axis=0)


def lag_sums(products, mask):
    out = []
    for h in range(2):
        part = products[:, h * HALF : (h + 1) * HALF].reshape(PAIRS, FILT, HALF) * mask[None]
        part = pltpu.roll(part.reshape(PAIRS * FILT, HALF), 1, 1, stride=1, stride_axis=0)
        out.append(jnp.sum(part.reshape(PAIRS, FILT, HALF), axis=1))
    return jnp.concatenate(out, axis=0)


def pick_groups(stacked):
    which = lane_group()
    out = stacked[:FILT]
    for p in range(1, PAIRS):
        out = jnp.where(which == p, stacked[p * FILT : (p + 1) * FILT], out)
    return out


def circulants(taps):
    rows = jnp.broadcast_to(taps[:, None, :], (PAIRS, FILT, HALF)).reshape(PAIRS * FILT, HALF)
    return pltpu.roll(rows, 0, 1, stride=1, stride_axis=0)


def correlate(x_back, mixed_two):
    return lax.dot_general(split_groups(x_back), mixed_two, (((1,), (1,)), ((), ())), preferred_element_type=F32)


def backwards_rows(rows):
    i = lax.broadcasted_iota(jnp.int32, (FILT, FILT), 0)
    j = lax.broadcasted_iota(jnp.int32, (FILT, FILT), 1)
    flip = (i + j == FILT - 1).astype(BF16)
    return jnp.dot(flip, rows, preferred_element_type=F32).astype(BF16)


def own_kernel(lens_ref, place_ref, mixed_ref, x_ref, taps_ref, lag_ref, down_ref, cross_ref, xb_ref, mask_ref):
    @pl.when(pl.program_id(0) == 0)
    def _():
        base = place_ref[0] * FILT
        own, cross = document_masks(lens_ref, base, False)
        mask_ref[0] = own.astype(F32)
        mask_ref[1] = cross.astype(F32)
        own_back, _ = document_masks(lens_ref, base, True)
        mask_ref[2] = own_back.astype(F32)

    mixed_two = two_halves(mixed_ref[...])
    x_back = backwards_rows(x_ref[...])
    xb_ref[...] = x_back
    lag_ref[...] = lag_sums(correlate(x_back, mixed_two), mask_ref[2])
    taps = taps_ref[...].astype(BF16).astype(F32)
    bands = [circulants(taps[h * PAIRS : (h + 1) * PAIRS]).reshape(PAIRS, FILT, HALF) for h in range(2)]
    for h in range(2):
        cross_ref[:, h * HALF : (h + 1) * HALF] = (bands[h] * mask_ref[1][None]).astype(BF16).reshape(PAIRS * FILT, HALF)
    own_band = jnp.concatenate(
        [(band * mask_ref[0][None]).astype(BF16).reshape(PAIRS * FILT, HALF) for band in bands], axis=1
    )
    down_ref[...] = pick_groups(jnp.dot(own_band, mixed_two, preferred_element_type=F32))


def own_part(lens, place, mixed, x, taps):
    channels = x.shape[1]
    tiles = channels // TILE
    groups = channels // GROUP
    smem = pl.BlockSpec(memory_space=pltpu.SMEM)
    wide = pl.BlockSpec((FILT, TILE), lambda t: (0, t))
    return pl.pallas_call(
        own_kernel,
        grid=(tiles,),
        in_specs=[smem, smem, wide, wide, pl.BlockSpec((2 * PAIRS, FILT), lambda t: (t, 0))],
        out_specs=[
            pl.BlockSpec((2 * PAIRS, FILT), lambda t: (t, 0)),
            wide,
            pl.BlockSpec((PAIRS * FILT, TILE), lambda t: (t, 0)),
            wide,
        ],
        out_shape=[
            jax.ShapeDtypeStruct((groups, FILT), F32),
            jax.ShapeDtypeStruct((FILT, channels), F32),
            jax.ShapeDtypeStruct((tiles * PAIRS * FILT, TILE), BF16),
            jax.ShapeDtypeStruct((FILT, channels), BF16),
        ],
        scratch_shapes=[pltpu.VMEM((3, FILT, HALF), F32)],
        compiler_params=pltpu.CompilerParams(vmem_limit_bytes=24 << 20),
        cost_estimate=pl.CostEstimate(flops=2 * 2 * FILT * TILE * TILE * tiles * PAIRS, bytes_accessed=16 << 20, transcendentals=0),
        name="own_part",
    )(lens, place, mixed, x, taps)


def lag_kernel(lens_ref, place_ref, halo_ref, xb_ref, lag_ref, out_ref):
    _, mask = document_masks(lens_ref, place_ref[0] * FILT, True)
    mask = mask.astype(F32)
    for t in range(halo_ref.shape[1] // TILE):
        lanes = slice(t * TILE, (t + 1) * TILE)
        rows = slice(t * 2 * PAIRS, (t + 1) * 2 * PAIRS)
        sums = lag_sums(correlate(xb_ref[:, lanes], two_halves(halo_ref[:, lanes])), mask)
        out_ref[rows] = lag_ref[rows] + sums


def lag_part(lens, place, halo, x_back, lag, piece):
    width = halo.shape[1]
    rows = width // GROUP
    smem = pl.BlockSpec(memory_space=pltpu.SMEM)
    return pl.pallas_call(
        lag_kernel,
        grid=(1,),
        in_specs=[
            smem,
            smem,
            pl.BlockSpec((FILT, width), lambda i: (0, 0)),
            pl.BlockSpec((FILT, width), lambda i: (0, piece)),
            pl.BlockSpec((rows, FILT), lambda i: (piece, 0)),
        ],
        out_specs=pl.BlockSpec((rows, FILT), lambda i: (0, 0)),
        out_shape=jax.ShapeDtypeStruct((rows, FILT), F32),
        compiler_params=pltpu.CompilerParams(vmem_limit_bytes=24 << 20),
        cost_estimate=pl.CostEstimate(flops=2 * FILT * TILE * width * PAIRS, bytes_accessed=2 << 20, transcendentals=0),
        name="lag_part",
    )(lens, place, halo, x_back, lag)


def down_kernel(*refs):
    halo_refs, (cross_ref, down_ref, out_ref) = refs[:-3], refs[-3:]
    pieces = len(halo_refs)
    here = pl.program_id(0) // (pl.num_programs(0) // pieces)
    halo = halo_refs[0][...]
    for k in range(1, pieces):
        halo = jnp.where(here == k, halo_refs[k][...], halo)
    picked = pick_groups(jnp.dot(cross_ref[...], two_halves(halo), preferred_element_type=F32))
    out_ref[...] = (down_ref[...] + picked).astype(BF16)


def down_part(halos, cross_band, down):
    channels = down.shape[1]
    tiles = channels // TILE
    each = tiles // len(halos)
    wide = pl.BlockSpec((FILT, TILE), lambda t: (0, t))
    return pl.pallas_call(
        down_kernel,
        grid=(tiles,),
        in_specs=[
            pl.BlockSpec((FILT, TILE), functools.partial(lambda k, t: (0, jnp.clip(t - k * each, 0, each - 1)), k))
            for k in range(len(halos))
        ]
        + [pl.BlockSpec((PAIRS * FILT, TILE), lambda t: (t, 0)), wide],
        out_specs=wide,
        out_shape=jax.ShapeDtypeStruct((FILT, channels), BF16),
        compiler_params=pltpu.CompilerParams(vmem_limit_bytes=24 << 20),
        cost_estimate=pl.CostEstimate(flops=2 * FILT * TILE * TILE * tiles * PAIRS, bytes_accessed=12 << 20, transcendentals=0),
        name="down_part",
    )(*halos, cross_band, down)


def shards(pieces, gate_branch, conv_input, grad_output, filter_taps, document_lengths):
    local_rows, channels = gate_branch.shape
    ctx_count = lax.axis_size("ctx")
    dp_count = lax.axis_size("dp")
    grad_scale = (1.0 * GROUP * dp_count * local_rows * ctx_count) ** (-0.5)
    place = lax.axis_index("ctx").astype(jnp.int32).reshape(1)
    mixed = (grad_output.astype(F32) * gate_branch.astype(F32)).astype(BF16)
    width = channels // pieces
    back = [(i, i - 1) for i in range(1, ctx_count)]
    halos = [lax.ppermute(mixed[:, k * width : (k + 1) * width], "ctx", back) for k in range(pieces)]
    lag, down, cross_band, x_back = own_part(document_lengths, place, mixed, conv_input, filter_taps)
    lags = [lag_part(document_lengths, place, halos[k], x_back, lag, k) for k in range(pieces)]
    partial = jnp.concatenate(lags * dp_count, axis=0).reshape(dp_count * ctx_count, -1, FILT)
    shared = lax.all_to_all(partial, ("dp", "ctx"), 0, 0, tiled=True)
    filter_grad = jnp.sum(shared, axis=0) * grad_scale
    grad_input = down_part(halos, cross_band, down)
    return grad_input, filter_grad


def solution(mesh):
    rows = P(("dp", "ctx"), None)
    return jax.shard_map(
        functools.partial(shards, 2),
        mesh=mesh,
        in_specs=(rows, rows, rows, P(), P("dp", None)),
        out_specs=(rows, P("ctx", None)),
        check_vma=False,
    )
```

```python
import functools

import jax
import jax.numpy as jnp
from jax import lax
from jax.experimental import pallas as pl
from jax.experimental.pallas import tpu as pltpu
from jax.sharding import PartitionSpec as P

GROUP = 16
FILT = 128
TILE = 256
HALF = 128
PAIRS = HALF // GROUP
BLOCK = 32
STEPS = FILT // BLOCK
BIG = 1 << 30
F32 = jnp.float32
BF16 = jnp.bfloat16
VMEM = pl.BlockSpec(memory_space=pltpu.VMEM)
SMEM = pl.BlockSpec(memory_space=pltpu.SMEM)


def iotas(shape):
    return lax.broadcasted_iota(jnp.int32, shape, 0), lax.broadcasted_iota(jnp.int32, shape, 1)


def own_mask(lens_ref, base, step, backwards):
    b, k = iotas((BLOCK, HALF))
    if backwards:
        b = BLOCK - 1 - b
    row = b + BLOCK * step
    limit = jnp.full((BLOCK, HALF), FILT, jnp.int32)
    end = -base
    for n in range(lens_ref.shape[1]):
        end = end + lens_ref[0, n]
        limit = jnp.minimum(limit, jnp.where(row < end, end, BIG))
    return row + ((k - b) & (FILT - 1)) < limit


def span(lens_ref, base):
    first, count = jnp.int32(-BIG), jnp.int32(BIG)
    end = -base
    for n in range(lens_ref.shape[1]):
        end = end + lens_ref[0, n]
        inside = end < FILT
        first = jnp.where(inside, end, first)
        count = jnp.where(inside, count, jnp.minimum(count, end - FILT))
    return first, count


def cross_fold(backwards):
    b, k = iotas((BLOCK, HALF))
    if backwards:
        b = BLOCK - 1 - b
    return (k >= BLOCK) | (k < b)


def halves(rows):
    lane = lax.broadcasted_iota(jnp.int32, rows.shape, 1)
    zero = jnp.zeros_like(rows)
    return jnp.where(lane < HALF, rows, zero), jnp.where(lane >= HALF, rows, zero)


def turned(rows, step):
    if step == 0:
        return rows
    return jnp.concatenate([rows[BLOCK * step :], rows[: BLOCK * step]], axis=0)


def turned_cross(rows, step):
    parts = [rows[BLOCK * step : BLOCK * (step + 1)]]
    if step < STEPS - 1:
        parts.append(jnp.zeros((BLOCK * (STEPS - 1 - step), rows.shape[1]), rows.dtype))
    if step > 0:
        parts.append(rows[: BLOCK * step])
    return jnp.concatenate(parts, axis=0)


def split_groups(rows):
    which = (lax.broadcasted_iota(jnp.int32, rows.shape, 1) % HALF) // GROUP
    zero = jnp.zeros_like(rows)
    return jnp.concatenate([jnp.where(which == p, rows, zero) for p in range(PAIRS)], axis=0)


def pick_groups(stacked):
    which = (lax.broadcasted_iota(jnp.int32, (BLOCK, TILE), 1) % HALF) // GROUP
    out = stacked[:BLOCK]
    for p in range(1, PAIRS):
        out = jnp.where(which == p, stacked[p * BLOCK : (p + 1) * BLOCK], out)
    return out


def correlate(x_back, step, stacked):
    at = STEPS - 1 - step
    rows = split_groups(x_back[BLOCK * at : BLOCK * (at + 1)])
    return lax.dot_general(rows, stacked, (((1,), (1,)), ((), ())), preferred_element_type=F32)


def lag_sums(total):
    out = []
    for h in range(2):
        for p in range(PAIRS):
            part = total[p * BLOCK : (p + 1) * BLOCK, h * HALF : (h + 1) * HALF]
            part = pltpu.roll(part, HALF - BLOCK + 1, 1, stride=1, stride_axis=0)
            out.append(jnp.sum(part, axis=0, keepdims=True))
    return jnp.concatenate(out, axis=0)


def bands(taps):
    out = []
    for h in range(2):
        groups = []
        for p in range(h * PAIRS, (h + 1) * PAIRS):
            rows = jnp.broadcast_to(taps[p : p + 1], (BLOCK, HALF))
            groups.append(pltpu.roll(rows, 0, 1, stride=1, stride_axis=0))
        out.append(jnp.concatenate(groups, axis=0))
    return jnp.concatenate(out, axis=1)


def backwards_rows(rows):
    i, j = iotas((FILT, FILT))
    flip = (i + j == FILT - 1).astype(BF16)
    return jnp.dot(flip, rows, preferred_element_type=F32).astype(BF16)


def tiled(mask):
    return jnp.concatenate([mask] * PAIRS, axis=0)


def own_kernel(pieces, *refs):
    lens_ref, place_ref = refs[:2]
    mixed_refs = refs[2 : 2 + pieces]
    x_ref, taps_ref, lag_ref, down_ref, band_ref, xb_ref, back_ref, ahead_ref = refs[2 + pieces :]
    base = place_ref[0] * FILT
    for step in range(STEPS):
        back_ref[step] = own_mask(lens_ref, base, step, True).astype(F32)
        ahead = own_mask(lens_ref, base, step, False).astype(F32).astype(BF16)
        ahead_ref[step] = jnp.concatenate([ahead, ahead], axis=1)
    fold = cross_fold(False).astype(F32).astype(BF16)
    fold = tiled(jnp.concatenate([fold, fold], axis=1))
    first, _ = span(lens_ref, base)
    row, _ = iotas((FILT, TILE))
    keep = (FILT - 1 - row >= first).astype(F32).astype(BF16)
    at = 0
    for mixed_ref in mixed_refs:
        for t in range(mixed_ref.shape[1] // TILE):
            lanes = slice(at * TILE, (at + 1) * TILE)
            groups = slice(at * 2 * PAIRS, (at + 1) * 2 * PAIRS)
            stack = slice(at * PAIRS * BLOCK, (at + 1) * PAIRS * BLOCK)
            at += 1
            low, high = halves(mixed_ref[:, t * TILE : (t + 1) * TILE])
            x_back = backwards_rows(x_ref[:, lanes])
            xb_ref[:, lanes] = x_back * keep
            band = bands(taps_ref[groups].astype(BF16).astype(F32)).astype(BF16)
            band_ref[stack] = band * fold
            total = None
            for step in range(STEPS):
                stacked = jnp.concatenate([turned(low, step), turned(high, step)], axis=0)
                product = correlate(x_back, step, stacked).reshape(PAIRS, BLOCK, TILE)
                mask = back_ref[step]
                product = product * jnp.concatenate([mask, mask], axis=1)[None]
                total = product if total is None else total + product
                down = jnp.dot(band * tiled(ahead_ref[step]), stacked, preferred_element_type=F32)
                down_ref[BLOCK * step : BLOCK * (step + 1), lanes] = pick_groups(down)
            lag_ref[groups] = lag_sums(total.reshape(PAIRS * BLOCK, TILE))


def own_part(lens, place, mixed, x, taps):
    channels = x.shape[1]
    tiles = channels // TILE
    return pl.pallas_call(
        functools.partial(own_kernel, len(mixed)),
        in_specs=[SMEM, SMEM] + [VMEM] * (len(mixed) + 2),
        out_specs=[VMEM] * 4,
        out_shape=[
            jax.ShapeDtypeStruct((channels // GROUP, FILT), F32),
            jax.ShapeDtypeStruct((FILT, channels), F32),
            jax.ShapeDtypeStruct((tiles * PAIRS * BLOCK, TILE), BF16),
            jax.ShapeDtypeStruct((FILT, channels), BF16),
        ],
        scratch_shapes=[pltpu.VMEM((STEPS, BLOCK, HALF), F32), pltpu.VMEM((STEPS, BLOCK, TILE), BF16)],
        compiler_params=pltpu.CompilerParams(vmem_limit_bytes=24 << 20),
        cost_estimate=pl.CostEstimate(flops=4 * FILT * TILE * TILE * tiles * PAIRS, bytes_accessed=8 << 20, transcendentals=0),
        name="own_part",
    )(lens, place, *mixed, x, taps)


def next_rows(count, halo):
    row, _ = iotas(halo.shape)
    return halves(halo * (row < count).astype(F32).astype(BF16))


def lag_kernel(first_group, scale, copies, *refs):
    lens_ref, place_ref, halo_ref, xb_ref, lag_ref = refs[:5]
    out_ref = refs[-1]
    earlier = refs[5:-1]
    _, count = span(lens_ref, place_ref[0] * FILT)
    fold = cross_fold(True).astype(F32)
    fold = tiled(jnp.concatenate([fold, fold], axis=1))
    if earlier:
        done = earlier[0][...]
        for c in range(copies):
            out_ref[c, :first_group] = done
    for t in range(halo_ref.shape[1] // TILE):
        low, high = next_rows(count, halo_ref[:, t * TILE : (t + 1) * TILE])
        at = first_group * GROUP + t * TILE
        total = None
        for step in range(STEPS):
            stacked = jnp.concatenate([turned_cross(low, step), turned_cross(high, step)], axis=0)
            product = correlate(xb_ref[:, at : at + TILE], step, stacked)
            total = product if total is None else total + product
        rows = first_group + t * 2 * PAIRS
        sums = (lag_ref[rows : rows + 2 * PAIRS] + lag_sums(total * fold)) * scale
        if copies:
            for c in range(copies):
                out_ref[c, rows : rows + 2 * PAIRS] = sums
        else:
            out_ref[rows : rows + 2 * PAIRS] = sums


def lag_part(lens, place, halo, x_back, lag, first_group, scale, copies, earlier):
    width = halo.shape[1]
    rows = first_group + width // GROUP
    shape = (copies, rows, FILT) if copies else (rows, FILT)
    return pl.pallas_call(
        functools.partial(lag_kernel, first_group, scale, copies),
        in_specs=[SMEM, SMEM] + [VMEM] * (3 + len(earlier)),
        out_specs=VMEM,
        out_shape=jax.ShapeDtypeStruct(shape, F32),
        compiler_params=pltpu.CompilerParams(vmem_limit_bytes=16 << 20),
        cost_estimate=pl.CostEstimate(flops=2 * FILT * TILE * width * PAIRS, bytes_accessed=2 << 20, transcendentals=0),
        name="lag_part",
    )(lens, place, halo, x_back, lag, *earlier)


def down_kernel(pieces, *refs):
    lens_ref, place_ref = refs[:2]
    halo_refs = refs[2 : 2 + pieces]
    band_ref, down_ref, out_ref, rows_ref, sems = refs[2 + pieces :]
    first, count = span(lens_ref, place_ref[0] * FILT)
    row, _ = iotas((BLOCK, TILE))
    at = 0
    copies = []
    for halo_ref in halo_refs:
        for t in range(halo_ref.shape[1] // TILE):
            lanes = slice(at * TILE, (at + 1) * TILE)
            low, high = next_rows(count, halo_ref[:, t * TILE : (t + 1) * TILE])
            band = band_ref[at * PAIRS * BLOCK : (at + 1) * PAIRS * BLOCK]
            for step in range(STEPS):
                stacked = jnp.concatenate([turned_cross(low, step), turned_cross(high, step)], axis=0)
                picked = pick_groups(jnp.dot(band, stacked, preferred_element_type=F32))
                rows = slice(BLOCK * step, BLOCK * (step + 1))
                picked = jnp.where(row + BLOCK * step >= first, picked, 0.0)
                rows_ref[rows, lanes] = (down_ref[rows, lanes] + picked).astype(BF16)
            copy = pltpu.make_async_copy(rows_ref.at[:, lanes], out_ref.at[:, lanes], sems.at[at])
            copy.start()
            copies.append(copy)
            at += 1
    for copy in copies:
        copy.wait()


def down_part(lens, place, halos, band, down):
    channels = down.shape[1]
    tiles = channels // TILE
    return pl.pallas_call(
        functools.partial(down_kernel, len(halos)),
        in_specs=[SMEM, SMEM] + [VMEM] * (len(halos) + 2),
        out_specs=pl.BlockSpec(memory_space=pl.ANY),
        out_shape=jax.ShapeDtypeStruct((FILT, channels), BF16),
        scratch_shapes=[pltpu.VMEM((FILT, channels), BF16), pltpu.SemaphoreType.DMA((tiles,))],
        compiler_params=pltpu.CompilerParams(vmem_limit_bytes=16 << 20),
        cost_estimate=pl.CostEstimate(flops=2 * FILT * TILE * TILE * tiles * PAIRS, bytes_accessed=4 << 20, transcendentals=0),
        name="down_part",
    )(lens, place, *halos, band, down)


def shards(gate_branch, conv_input, grad_output, filter_taps, document_lengths):
    local_rows, channels = gate_branch.shape
    ctx_count = lax.axis_size("ctx")
    dp_count = lax.axis_size("dp")
    grad_scale = (1.0 * GROUP * dp_count * local_rows * ctx_count) ** (-0.5)
    place = lax.axis_index("ctx").astype(jnp.int32).reshape(1)
    cuts = [0, channels // 2, channels]
    back = [(i, i - 1) for i in range(1, ctx_count)]
    mixed, halos = [], []
    for low, high in zip(cuts, cuts[1:]):
        gate, grad = gate_branch[:, low:high], grad_output[:, low:high]
        mixed.append((grad.astype(F32) * gate.astype(F32)).astype(BF16))
        halos.append(lax.ppermute(mixed[-1], "ctx", back))
    lag, down, band, x_back = own_part(document_lengths, place, mixed, conv_input, filter_taps)
    sums = []
    for k in range(len(halos)):
        copies = dp_count if k == len(halos) - 1 else 0
        sums = [lag_part(document_lengths, place, halos[k], x_back, lag, cuts[k] // GROUP, grad_scale, copies, sums)]
    partial = sums[0].reshape(dp_count * ctx_count, -1, FILT)
    shared = lax.all_to_all(partial, ("dp", "ctx"), 0, 0, tiled=True)
    filter_grad = jnp.sum(shared, axis=0)
    grad_input = down_part(document_lengths, place, halos, band, down)
    return grad_input, filter_grad


def solution(mesh):
    rows = P(("dp", "ctx"), None)
    return jax.shard_map(
        shards,
        mesh=mesh,
        in_specs=(rows, rows, rows, P(), P("dp", None)),
        out_specs=(rows, P("ctx", None)),
        check_vma=False,
    )
```

```python
import functools

import jax
import jax.numpy as jnp
from jax import lax
from jax.experimental import pallas as pl
from jax.experimental.pallas import tpu as pltpu
from jax.sharding import PartitionSpec as P

GROUP = 16
FILT = 128
TILE = 256
HALF = 128
PAIRS = HALF // GROUP
BLOCK = 32
STEPS = FILT // BLOCK
BIG = 1 << 30
F32 = jnp.float32
BF16 = jnp.bfloat16
SENT = jnp.bfloat16
VMEM = pl.BlockSpec(memory_space=pltpu.VMEM)
SMEM = pl.BlockSpec(memory_space=pltpu.SMEM)


def iotas(shape):
    return lax.broadcasted_iota(jnp.int32, shape, 0), lax.broadcasted_iota(jnp.int32, shape, 1)


def own_mask(lens_ref, base, step, backwards):
    b, k = iotas((BLOCK, HALF))
    if backwards:
        b = BLOCK - 1 - b
    row = b + BLOCK * step
    limit = jnp.full((BLOCK, HALF), FILT, jnp.int32)
    end = -base
    for n in range(lens_ref.shape[1]):
        end = end + lens_ref[0, n]
        limit = jnp.minimum(limit, jnp.where(row < end, end, BIG))
    return row + ((k - b) & (FILT - 1)) < limit


def span(lens_ref, base):
    first, count = jnp.int32(-BIG), jnp.int32(BIG)
    end = -base
    for n in range(lens_ref.shape[1]):
        end = end + lens_ref[0, n]
        inside = end < FILT
        first = jnp.where(inside, end, first)
        count = jnp.where(inside, count, jnp.minimum(count, end - FILT))
    return first, count


def cross_fold(backwards):
    b, k = iotas((BLOCK, HALF))
    if backwards:
        b = BLOCK - 1 - b
    return (k >= BLOCK) | (k < b)


def halves(rows):
    lane = lax.broadcasted_iota(jnp.int32, rows.shape, 1)
    zero = jnp.zeros_like(rows)
    return jnp.where(lane < HALF, rows, zero), jnp.where(lane >= HALF, rows, zero)


def turned(rows, step):
    if step == 0:
        return rows
    return jnp.concatenate([rows[BLOCK * step :], rows[: BLOCK * step]], axis=0)


def turned_cross(rows, step):
    parts = [rows[BLOCK * step : BLOCK * (step + 1)]]
    if step < STEPS - 1:
        parts.append(jnp.zeros((BLOCK * (STEPS - 1 - step), rows.shape[1]), rows.dtype))
    if step > 0:
        parts.append(rows[: BLOCK * step])
    return jnp.concatenate(parts, axis=0)


def split_groups(rows):
    which = (lax.broadcasted_iota(jnp.int32, rows.shape, 1) % HALF) // GROUP
    zero = jnp.zeros_like(rows)
    return jnp.concatenate([jnp.where(which == p, rows, zero) for p in range(PAIRS)], axis=0)


def pick_groups(stacked):
    which = (lax.broadcasted_iota(jnp.int32, (BLOCK, TILE), 1) % HALF) // GROUP
    out = stacked[:BLOCK]
    for p in range(1, PAIRS):
        out = jnp.where(which == p, stacked[p * BLOCK : (p + 1) * BLOCK], out)
    return out


def correlate(x_back, step, stacked):
    at = STEPS - 1 - step
    rows = split_groups(x_back[BLOCK * at : BLOCK * (at + 1)])
    return lax.dot_general(rows, stacked, (((1,), (1,)), ((), ())), preferred_element_type=F32)


def lag_sums(total):
    out = []
    for h in range(2):
        for p in range(PAIRS):
            part = total[p * BLOCK : (p + 1) * BLOCK, h * HALF : (h + 1) * HALF]
            part = pltpu.roll(part, HALF - BLOCK + 1, 1, stride=1, stride_axis=0)
            out.append(jnp.sum(part, axis=0, keepdims=True))
    return jnp.concatenate(out, axis=0)


def bands(taps):
    out = []
    for h in range(2):
        groups = []
        for p in range(h * PAIRS, (h + 1) * PAIRS):
            rows = jnp.broadcast_to(taps[p : p + 1], (BLOCK, HALF))
            groups.append(pltpu.roll(rows, 0, 1, stride=1, stride_axis=0))
        out.append(jnp.concatenate(groups, axis=0))
    return jnp.concatenate(out, axis=1)


def backwards_rows(rows):
    i, j = iotas((FILT, FILT))
    flip = (i + j == FILT - 1).astype(BF16)
    return jnp.dot(flip, rows, preferred_element_type=F32).astype(BF16)


def tiled(mask):
    return jnp.concatenate([mask] * PAIRS, axis=0)


def own_kernel(pieces, *refs):
    lens_ref, place_ref = refs[:2]
    mixed_refs = refs[2 : 2 + pieces]
    x_ref, lag_ref, xb_ref, keep_ref, mask_ref, back_ref = refs[2 + pieces :]
    base = place_ref[0] * FILT
    first, count = span(lens_ref, base)
    row, _ = iotas((FILT, TILE))
    keep_ref[0] = (FILT - 1 - row >= first).astype(F32).astype(BF16)
    keep_ref[1] = (row < count).astype(F32).astype(BF16)
    row, _ = iotas((BLOCK, HALF))
    for step in range(STEPS):
        back = own_mask(lens_ref, base, step, True).astype(F32)
        back_ref[step] = jnp.concatenate([back, back], axis=1)
        ahead = own_mask(lens_ref, base, step, False)
        cross = cross_fold(False) & (row + BLOCK * step >= first)
        masks = [mask.astype(F32).astype(BF16) for mask in (ahead, ahead, cross, cross)]
        mask_ref[step] = jnp.concatenate(masks, axis=1)
    tiles = []
    for k in range(pieces):
        for t in range(mixed_refs[k].shape[1] // TILE):
            tiles.append((len(tiles), k, t))
    for at, _, _ in tiles:
        lanes = slice(at * TILE, (at + 1) * TILE)
        xb_ref[:, lanes] = backwards_rows(x_ref[:, lanes])
    for at, k, t in tiles:
        groups = slice(at * 2 * PAIRS, (at + 1) * 2 * PAIRS)
        low, high = halves(mixed_refs[k][:, t * TILE : (t + 1) * TILE])
        x_back = xb_ref[:, at * TILE : (at + 1) * TILE]
        total = None
        for step in range(STEPS):
            stacked = jnp.concatenate([turned(low, step), turned(high, step)], axis=0)
            product = correlate(x_back, step, stacked).reshape(PAIRS, BLOCK, TILE) * back_ref[step][None]
            total = product if total is None else total + product
        lag_ref[groups] = lag_sums(total.reshape(PAIRS * BLOCK, TILE))


def own_part(lens, place, mixed, x):
    channels = x.shape[1]
    pieces = len(mixed)
    return pl.pallas_call(
        functools.partial(own_kernel, pieces),
        in_specs=[SMEM, SMEM] + [VMEM] * (pieces + 1),
        out_specs=[VMEM] * 4,
        out_shape=[
            jax.ShapeDtypeStruct((channels // GROUP, FILT), F32),
            jax.ShapeDtypeStruct((FILT, channels), BF16),
            jax.ShapeDtypeStruct((2, FILT, TILE), BF16),
            jax.ShapeDtypeStruct((STEPS, BLOCK, 2 * TILE), BF16),
        ],
        scratch_shapes=[pltpu.VMEM((STEPS, BLOCK, TILE), F32)],
        compiler_params=pltpu.CompilerParams(vmem_limit_bytes=16 << 20),
        cost_estimate=pl.CostEstimate(flops=2 * FILT * TILE * channels * PAIRS, bytes_accessed=4 << 20, transcendentals=0),
        name="own_part",
    )(lens, place, *mixed, x)


def lag_kernel(first_group, scale, copies, *refs):
    keep_ref, halo_ref, xb_ref, lag_ref = refs[:4]
    out_ref = refs[-1]
    earlier = refs[4:-1]
    fold = cross_fold(True).astype(F32)
    fold = tiled(jnp.concatenate([fold, fold], axis=1))
    if earlier:
        done = earlier[0][...].astype(out_ref.dtype)
        for c in range(copies):
            out_ref[c, :first_group] = done
    for t in range(halo_ref.shape[1] // TILE):
        low, high = halves(halo_ref[:, t * TILE : (t + 1) * TILE] * keep_ref[1])
        at = first_group * GROUP + t * TILE
        x_back = xb_ref[:, at : at + TILE] * keep_ref[0]
        total = None
        for step in range(STEPS):
            stacked = jnp.concatenate([turned_cross(low, step), turned_cross(high, step)], axis=0)
            product = correlate(x_back, step, stacked)
            total = product if total is None else total + product
        rows = first_group + t * 2 * PAIRS
        sums = (lag_ref[rows : rows + 2 * PAIRS] + lag_sums(total * fold)) * scale
        if copies:
            for c in range(copies):
                out_ref[c, rows : rows + 2 * PAIRS] = sums.astype(out_ref.dtype)
        else:
            out_ref[rows : rows + 2 * PAIRS] = sums


def lag_part(keep, halo, x_back, lag, first_group, scale, copies, earlier):
    width = halo.shape[1]
    rows = first_group + width // GROUP
    shape = jax.ShapeDtypeStruct((copies, rows, FILT), SENT) if copies else jax.ShapeDtypeStruct((rows, FILT), F32)
    return pl.pallas_call(
        functools.partial(lag_kernel, first_group, scale, copies),
        in_specs=[VMEM] * (4 + len(earlier)),
        out_specs=VMEM,
        out_shape=shape,
        compiler_params=pltpu.CompilerParams(vmem_limit_bytes=16 << 20),
        cost_estimate=pl.CostEstimate(flops=2 * FILT * TILE * width * PAIRS, bytes_accessed=2 << 20, transcendentals=0),
        name="lag_part",
    )(keep, halo, x_back, lag, *earlier)


def down_kernel(pieces, *refs):
    keep_ref, mask_ref, taps_ref = refs[:3]
    mixed_refs = refs[3 : 3 + pieces]
    halo_refs = refs[3 + pieces : 3 + 2 * pieces]
    out_ref, band_ref, rows_ref, sems = refs[3 + 2 * pieces :]
    tiles = []
    for k in range(pieces):
        for t in range(mixed_refs[k].shape[1] // TILE):
            tiles.append((len(tiles), k, t))
    for at, _, _ in tiles:
        taps = taps_ref[at * 2 * PAIRS : (at + 1) * 2 * PAIRS].astype(BF16).astype(F32)
        band_ref[at * PAIRS * BLOCK : (at + 1) * PAIRS * BLOCK] = bands(taps).astype(BF16)
    copies = []
    for at, k, t in tiles:
        lanes = slice(t * TILE, (t + 1) * TILE)
        low, high = halves(mixed_refs[k][:, lanes])
        next_low, next_high = halves(halo_refs[k][:, lanes] * keep_ref[1])
        band = band_ref[at * PAIRS * BLOCK : (at + 1) * PAIRS * BLOCK]
        band = jnp.concatenate([band, band], axis=1)
        for step in range(STEPS):
            stacked = [turned(low, step), turned(high, step), turned_cross(next_low, step), turned_cross(next_high, step)]
            stacked = jnp.concatenate(stacked, axis=0)
            product = jnp.dot(band * tiled(mask_ref[step]), stacked, preferred_element_type=F32)
            rows_ref[BLOCK * step : BLOCK * (step + 1), at * TILE : (at + 1) * TILE] = pick_groups(product).astype(BF16)
        lanes = slice(at * TILE, (at + 1) * TILE)
        copy = pltpu.make_async_copy(rows_ref.at[:, lanes], out_ref.at[:, lanes], sems.at[at])
        copy.start()
        copies.append(copy)
    for copy in copies:
        copy.wait()


def down_part(keep, masks, taps, mixed, halos):
    pieces = len(mixed)
    channels = taps.shape[0] * GROUP
    tiles = channels // TILE
    return pl.pallas_call(
        functools.partial(down_kernel, pieces),
        in_specs=[VMEM] * (3 + 2 * pieces),
        out_specs=pl.BlockSpec(memory_space=pl.ANY),
        out_shape=jax.ShapeDtypeStruct((FILT, channels), BF16),
        scratch_shapes=[
            pltpu.VMEM((tiles * PAIRS * BLOCK, TILE), BF16),
            pltpu.VMEM((FILT, channels), BF16),
            pltpu.SemaphoreType.DMA((tiles,)),
        ],
        compiler_params=pltpu.CompilerParams(vmem_limit_bytes=16 << 20),
        cost_estimate=pl.CostEstimate(flops=4 * FILT * TILE * channels * PAIRS, bytes_accessed=4 << 20, transcendentals=0),
        name="down_part",
    )(keep, masks, taps, *mixed, *halos)


def shards(gate_branch, conv_input, grad_output, filter_taps, document_lengths):
    local_rows, channels = gate_branch.shape
    ctx_count = lax.axis_size("ctx")
    dp_count = lax.axis_size("dp")
    grad_scale = (1.0 * GROUP * dp_count * local_rows * ctx_count) ** (-0.5)
    place = lax.axis_index("ctx").astype(jnp.int32).reshape(1)
    cuts = [0, channels * 5 // 8, channels]
    back = [(i, i - 1) for i in range(1, ctx_count)]
    mixed, halos = [], []
    gate, grad = gate_branch, grad_output
    for low, high in zip(cuts, cuts[1:]):
        if mixed:
            gate, grad, mixed[-1] = lax.optimization_barrier((gate, grad, mixed[-1]))
        mixed.append((grad[:, low:high].astype(F32) * gate[:, low:high].astype(F32)).astype(BF16))
        halos.append(lax.ppermute(mixed[-1], "ctx", back))
    pieces = len(mixed)
    lag, x_back, keep, masks = own_part(document_lengths, place, mixed, conv_input)
    sums = []
    for k in range(pieces):
        copies = dp_count if k == pieces - 1 else 0
        sums = [lag_part(keep, halos[k], x_back, lag, cuts[k] // GROUP, grad_scale, copies, sums)]
    partial = sums[0].reshape(dp_count * ctx_count, -1, FILT)
    shared = lax.all_to_all(partial, ("dp", "ctx"), 0, 0, tiled=True)
    filter_grad = jnp.sum(shared.astype(F32), axis=0)
    grad_input = down_part(keep, masks, filter_taps, mixed, halos)
    return grad_input, filter_grad


def solution(mesh):
    rows = P(("dp", "ctx"), None)
    return jax.shard_map(
        shards,
        mesh=mesh,
        in_specs=(rows, rows, rows, P(), P("dp", None)),
        out_specs=(rows, P("ctx", None)),
        check_vma=False,
    )
```

```python
import functools

import jax
import jax.numpy as jnp
from jax import lax
from jax.experimental import pallas as pl
from jax.experimental.pallas import tpu as pltpu
from jax.sharding import PartitionSpec as P

GROUP = 16
FILT = 128
TILE = 256
HALF = 128
PAIRS = HALF // GROUP
BLOCK = 32
STEPS = FILT // BLOCK
BIG = 1 << 30
F32 = jnp.float32
BF16 = jnp.bfloat16
SENT = jnp.bfloat16
VMEM = pl.BlockSpec(memory_space=pltpu.VMEM)
SMEM = pl.BlockSpec(memory_space=pltpu.SMEM)


def iotas(shape):
    return lax.broadcasted_iota(jnp.int32, shape, 0), lax.broadcasted_iota(jnp.int32, shape, 1)


def own_mask(lens_ref, base, step, backwards):
    b, k = iotas((BLOCK, HALF))
    if backwards:
        b = BLOCK - 1 - b
    row = b + BLOCK * step
    limit = jnp.full((BLOCK, HALF), FILT, jnp.int32)
    end = -base
    for n in range(lens_ref.shape[1]):
        end = end + lens_ref[0, n]
        limit = jnp.minimum(limit, jnp.where(row < end, end, BIG))
    return row + ((k - b) & (FILT - 1)) < limit


def span(lens_ref, base):
    first, count = jnp.int32(-BIG), jnp.int32(BIG)
    end = -base
    for n in range(lens_ref.shape[1]):
        end = end + lens_ref[0, n]
        inside = end < FILT
        first = jnp.where(inside, end, first)
        count = jnp.where(inside, count, jnp.minimum(count, end - FILT))
    return first, count


def cross_fold(backwards):
    b, k = iotas((BLOCK, HALF))
    if backwards:
        b = BLOCK - 1 - b
    return (k >= BLOCK) | (k < b)


def halves(rows):
    lane = lax.broadcasted_iota(jnp.int32, rows.shape, 1)
    zero = jnp.zeros_like(rows)
    return jnp.where(lane < HALF, rows, zero), jnp.where(lane >= HALF, rows, zero)


def turned(rows, step):
    if step == 0:
        return rows
    return jnp.concatenate([rows[BLOCK * step :], rows[: BLOCK * step]], axis=0)


def turned_cross(rows, step):
    parts = [rows[BLOCK * step : BLOCK * (step + 1)]]
    if step < STEPS - 1:
        parts.append(jnp.zeros((BLOCK * (STEPS - 1 - step), rows.shape[1]), rows.dtype))
    if step > 0:
        parts.append(rows[: BLOCK * step])
    return jnp.concatenate(parts, axis=0)


def split_groups(rows):
    which = (lax.broadcasted_iota(jnp.int32, rows.shape, 1) % HALF) // GROUP
    zero = jnp.zeros_like(rows)
    return jnp.concatenate([jnp.where(which == p, rows, zero) for p in range(PAIRS)], axis=0)


def pick_groups(stacked):
    which = (lax.broadcasted_iota(jnp.int32, (BLOCK, TILE), 1) % HALF) // GROUP
    out = stacked[:BLOCK]
    for p in range(1, PAIRS):
        out = jnp.where(which == p, stacked[p * BLOCK : (p + 1) * BLOCK], out)
    return out


def correlate(x_back, step, stacked):
    at = STEPS - 1 - step
    rows = split_groups(x_back[BLOCK * at : BLOCK * (at + 1)])
    return lax.dot_general(rows, stacked, (((1,), (1,)), ((), ())), preferred_element_type=F32)


def lag_sums(total):
    out = []
    for h in range(2):
        for p in range(PAIRS):
            part = total[p * BLOCK : (p + 1) * BLOCK, h * HALF : (h + 1) * HALF]
            part = pltpu.roll(part, HALF - BLOCK + 1, 1, stride=1, stride_axis=0)
            out.append(jnp.sum(part, axis=0, keepdims=True))
    return jnp.concatenate(out, axis=0)


def bands(taps):
    out = []
    for h in range(2):
        groups = []
        for p in range(h * PAIRS, (h + 1) * PAIRS):
            rows = jnp.broadcast_to(taps[p : p + 1], (BLOCK, HALF))
            groups.append(pltpu.roll(rows, 0, 1, stride=1, stride_axis=0))
        out.append(jnp.concatenate(groups, axis=0))
    return jnp.concatenate(out, axis=1)


def backwards_rows(rows):
    i, j = iotas((FILT, FILT))
    flip = (i + j == FILT - 1).astype(BF16)
    return jnp.dot(flip, rows, preferred_element_type=F32).astype(BF16)


def tiled(mask):
    return jnp.concatenate([mask] * PAIRS, axis=0)


def own_kernel(pieces, *refs):
    lens_ref, place_ref = refs[:2]
    mixed_refs = refs[2 : 2 + pieces]
    x_ref, lag_ref, xb_ref, keep_ref, mask_ref, back_ref = refs[2 + pieces :]
    base = place_ref[0] * FILT
    first, count = span(lens_ref, base)
    row, _ = iotas((FILT, TILE))
    keep_ref[0] = (FILT - 1 - row >= first).astype(F32).astype(BF16)
    keep_ref[1] = (row < count).astype(F32).astype(BF16)
    row, _ = iotas((BLOCK, HALF))
    for step in range(STEPS):
        back = own_mask(lens_ref, base, step, True).astype(F32)
        back_ref[step] = jnp.concatenate([back, back], axis=1)
        ahead = own_mask(lens_ref, base, step, False)
        cross = cross_fold(False) & (row + BLOCK * step >= first)
        masks = [mask.astype(F32).astype(BF16) for mask in (ahead, ahead, cross, cross)]
        mask_ref[step] = jnp.concatenate(masks, axis=1)
    tiles = []
    for k in range(pieces):
        for t in range(mixed_refs[k].shape[1] // TILE):
            tiles.append((len(tiles), k, t))
    for at, _, _ in tiles:
        lanes = slice(at * TILE, (at + 1) * TILE)
        xb_ref[:, lanes] = backwards_rows(x_ref[:, lanes])
    for at, k, t in tiles:
        groups = slice(at * 2 * PAIRS, (at + 1) * 2 * PAIRS)
        low, high = halves(mixed_refs[k][:, t * TILE : (t + 1) * TILE])
        x_back = xb_ref[:, at * TILE : (at + 1) * TILE]
        total = None
        for step in range(STEPS):
            stacked = jnp.concatenate([turned(low, step), turned(high, step)], axis=0)
            product = correlate(x_back, step, stacked).reshape(PAIRS, BLOCK, TILE) * back_ref[step][None]
            total = product if total is None else total + product
        lag_ref[groups] = lag_sums(total.reshape(PAIRS * BLOCK, TILE))


def own_part(lens, place, mixed, x):
    channels = x.shape[1]
    pieces = len(mixed)
    return pl.pallas_call(
        functools.partial(own_kernel, pieces),
        in_specs=[SMEM, SMEM] + [VMEM] * (pieces + 1),
        out_specs=[VMEM] * 4,
        out_shape=[
            jax.ShapeDtypeStruct((channels // GROUP, FILT), F32),
            jax.ShapeDtypeStruct((FILT, channels), BF16),
            jax.ShapeDtypeStruct((2, FILT, TILE), BF16),
            jax.ShapeDtypeStruct((STEPS, BLOCK, 2 * TILE), BF16),
        ],
        scratch_shapes=[pltpu.VMEM((STEPS, BLOCK, TILE), F32)],
        compiler_params=pltpu.CompilerParams(vmem_limit_bytes=16 << 20),
        cost_estimate=pl.CostEstimate(flops=2 * FILT * TILE * channels * PAIRS, bytes_accessed=4 << 20, transcendentals=0),
        name="own_part",
    )(lens, place, *mixed, x)


def lag_kernel(first_group, scale, copies, *refs):
    keep_ref, halo_ref, xb_ref, lag_ref = refs[:4]
    out_ref = refs[-1]
    earlier = refs[4:-1]
    fold = cross_fold(True).astype(F32)
    fold = tiled(jnp.concatenate([fold, fold], axis=1))
    if earlier:
        done = earlier[0][...].astype(out_ref.dtype)
        if copies:
            for c in range(copies):
                out_ref[c, :first_group] = done
        else:
            out_ref[:first_group] = done
    for t in range(halo_ref.shape[1] // TILE):
        low, high = halves(halo_ref[:, t * TILE : (t + 1) * TILE] * keep_ref[1])
        at = first_group * GROUP + t * TILE
        x_back = xb_ref[:, at : at + TILE] * keep_ref[0]
        total = None
        for step in range(STEPS):
            stacked = jnp.concatenate([turned_cross(low, step), turned_cross(high, step)], axis=0)
            product = correlate(x_back, step, stacked)
            total = product if total is None else total + product
        rows = first_group + t * 2 * PAIRS
        sums = (lag_ref[rows : rows + 2 * PAIRS] + lag_sums(total * fold)) * scale
        if copies:
            for c in range(copies):
                out_ref[c, rows : rows + 2 * PAIRS] = sums.astype(out_ref.dtype)
        else:
            out_ref[rows : rows + 2 * PAIRS] = sums


def lag_part(keep, halo, x_back, lag, first_group, scale, copies, earlier):
    width = halo.shape[1]
    rows = first_group + width // GROUP
    shape = jax.ShapeDtypeStruct((copies, rows, FILT), SENT) if copies else jax.ShapeDtypeStruct((rows, FILT), F32)
    return pl.pallas_call(
        functools.partial(lag_kernel, first_group, scale, copies),
        in_specs=[VMEM] * (4 + len(earlier)),
        out_specs=VMEM,
        out_shape=shape,
        compiler_params=pltpu.CompilerParams(vmem_limit_bytes=16 << 20),
        cost_estimate=pl.CostEstimate(flops=2 * FILT * TILE * width * PAIRS, bytes_accessed=2 << 20, transcendentals=0),
        name="lag_part",
    )(keep, halo, x_back, lag, *earlier)


def down_kernel(pieces, *refs):
    keep_ref, mask_ref, taps_ref = refs[:3]
    mixed_refs = refs[3 : 3 + pieces]
    halo_refs = refs[3 + pieces : 3 + 2 * pieces]
    out_ref, band_ref, rows_ref, sems = refs[3 + 2 * pieces :]
    tiles = []
    for k in range(pieces):
        for t in range(mixed_refs[k].shape[1] // TILE):
            tiles.append((len(tiles), k, t))
    for at, _, _ in tiles:
        taps = taps_ref[at * 2 * PAIRS : (at + 1) * 2 * PAIRS].astype(BF16).astype(F32)
        band_ref[at * PAIRS * BLOCK : (at + 1) * PAIRS * BLOCK] = bands(taps).astype(BF16)
    copies = []
    for at, k, t in tiles:
        lanes = slice(t * TILE, (t + 1) * TILE)
        low, high = halves(mixed_refs[k][:, lanes])
        next_low, next_high = halves(halo_refs[k][:, lanes] * keep_ref[1])
        band = band_ref[at * PAIRS * BLOCK : (at + 1) * PAIRS * BLOCK]
        band = jnp.concatenate([band, band], axis=1)
        for step in range(STEPS):
            stacked = [turned(low, step), turned(high, step), turned_cross(next_low, step), turned_cross(next_high, step)]
            stacked = jnp.concatenate(stacked, axis=0)
            product = jnp.dot(band * tiled(mask_ref[step]), stacked, preferred_element_type=F32)
            rows_ref[BLOCK * step : BLOCK * (step + 1), at * TILE : (at + 1) * TILE] = pick_groups(product).astype(BF16)
        lanes = slice(at * TILE, (at + 1) * TILE)
        copy = pltpu.make_async_copy(rows_ref.at[:, lanes], out_ref.at[:, lanes], sems.at[at])
        copy.start()
        copies.append(copy)
    for copy in copies:
        copy.wait()


def down_part(keep, masks, taps, mixed, halos):
    pieces = len(mixed)
    channels = taps.shape[0] * GROUP
    tiles = channels // TILE
    return pl.pallas_call(
        functools.partial(down_kernel, pieces),
        in_specs=[VMEM] * (3 + 2 * pieces),
        out_specs=pl.BlockSpec(memory_space=pl.ANY),
        out_shape=jax.ShapeDtypeStruct((FILT, channels), BF16),
        scratch_shapes=[
            pltpu.VMEM((tiles * PAIRS * BLOCK, TILE), BF16),
            pltpu.VMEM((FILT, channels), BF16),
            pltpu.SemaphoreType.DMA((tiles,)),
        ],
        compiler_params=pltpu.CompilerParams(vmem_limit_bytes=16 << 20),
        cost_estimate=pl.CostEstimate(flops=4 * FILT * TILE * channels * PAIRS, bytes_accessed=4 << 20, transcendentals=0),
        name="down_part",
    )(keep, masks, taps, *mixed, *halos)


def shards(gate_branch, conv_input, grad_output, filter_taps, document_lengths):
    local_rows, channels = gate_branch.shape
    ctx_count = lax.axis_size("ctx")
    dp_count = lax.axis_size("dp")
    grad_scale = (1.0 * GROUP * dp_count * local_rows * ctx_count) ** (-0.5)
    place = lax.axis_index("ctx").astype(jnp.int32).reshape(1)
    cuts = [0, channels * 5 // 8, channels * 7 // 8, channels]
    back = [(i, i - 1) for i in range(1, ctx_count)]
    mixed, halos = [], []
    gate, grad = gate_branch, grad_output
    for low, high in zip(cuts, cuts[1:]):
        if len(mixed) == 1:
            gate, grad, mixed[-1] = lax.optimization_barrier((gate, grad, mixed[-1]))
        mixed.append((grad[:, low:high].astype(F32) * gate[:, low:high].astype(F32)).astype(BF16))
        halos.append(lax.ppermute(mixed[-1], "ctx", back))
    pieces = len(mixed)
    lag, x_back, keep, masks = own_part(document_lengths, place, mixed, conv_input)
    sums = []
    for k in range(pieces):
        copies = dp_count if k == pieces - 1 else 0
        sums = [lag_part(keep, halos[k], x_back, lag, cuts[k] // GROUP, grad_scale, copies, sums)]
    partial = sums[0].reshape(dp_count * ctx_count, -1, FILT)
    shared = lax.all_to_all(partial, ("dp", "ctx"), 0, 0, tiled=True)
    filter_grad = jnp.sum(shared.astype(F32), axis=0)
    grad_input = down_part(keep, masks, filter_taps, mixed, halos)
    return grad_input, filter_grad


def solution(mesh):
    rows = P(("dp", "ctx"), None)
    return jax.shard_map(
        shards,
        mesh=mesh,
        in_specs=(rows, rows, rows, P(), P("dp", None)),
        out_specs=(rows, P("ctx", None)),
        check_vma=False,
    )
```

```python
import functools

import jax
import jax.numpy as jnp
from jax import lax
from jax.experimental import pallas as pl
from jax.experimental.pallas import tpu as pltpu
from jax.sharding import PartitionSpec as P

GROUP = 16
FILT = 128
TILE = 256
HALF = 128
PAIRS = HALF // GROUP
BLOCK = 32
STEPS = FILT // BLOCK
BIG = 1 << 30
F32 = jnp.float32
BF16 = jnp.bfloat16
SENT = jnp.bfloat16
VMEM = pl.BlockSpec(memory_space=pltpu.VMEM)
SMEM = pl.BlockSpec(memory_space=pltpu.SMEM)


def iotas(shape):
    return lax.broadcasted_iota(jnp.int32, shape, 0), lax.broadcasted_iota(jnp.int32, shape, 1)


def own_mask(lens_ref, base, step, backwards):
    b, k = iotas((BLOCK, HALF))
    if backwards:
        b = BLOCK - 1 - b
    row = b + BLOCK * step
    limit = jnp.full((BLOCK, HALF), FILT, jnp.int32)
    end = -base
    for n in range(lens_ref.shape[1]):
        end = end + lens_ref[0, n]
        limit = jnp.minimum(limit, jnp.where(row < end, end, BIG))
    return row + ((k - b) & (FILT - 1)) < limit


def span(lens_ref, base):
    first, count = jnp.int32(-BIG), jnp.int32(BIG)
    end = -base
    for n in range(lens_ref.shape[1]):
        end = end + lens_ref[0, n]
        inside = end < FILT
        first = jnp.where(inside, end, first)
        count = jnp.where(inside, count, jnp.minimum(count, end - FILT))
    return first, count


def cross_fold(backwards):
    b, k = iotas((BLOCK, HALF))
    if backwards:
        b = BLOCK - 1 - b
    return (k >= BLOCK) | (k < b)


def halves(rows):
    lane = lax.broadcasted_iota(jnp.int32, rows.shape, 1)
    zero = jnp.zeros_like(rows)
    return jnp.where(lane < HALF, rows, zero), jnp.where(lane >= HALF, rows, zero)


def turned(rows, step):
    if step == 0:
        return rows
    return jnp.concatenate([rows[BLOCK * step :], rows[: BLOCK * step]], axis=0)


def turned_cross(rows, step):
    parts = [rows[BLOCK * step : BLOCK * (step + 1)]]
    if step < STEPS - 1:
        parts.append(jnp.zeros((BLOCK * (STEPS - 1 - step), rows.shape[1]), rows.dtype))
    if step > 0:
        parts.append(rows[: BLOCK * step])
    return jnp.concatenate(parts, axis=0)


def split_groups(rows):
    which = (lax.broadcasted_iota(jnp.int32, rows.shape, 1) % HALF) // GROUP
    zero = jnp.zeros_like(rows)
    return jnp.concatenate([jnp.where(which == p, rows, zero) for p in range(PAIRS)], axis=0)


def pick_groups(stacked):
    which = (lax.broadcasted_iota(jnp.int32, (BLOCK, TILE), 1) % HALF) // GROUP
    out = stacked[:BLOCK]
    for p in range(1, PAIRS):
        out = jnp.where(which == p, stacked[p * BLOCK : (p + 1) * BLOCK], out)
    return out


def correlate(x_back, step, stacked):
    at = STEPS - 1 - step
    rows = split_groups(x_back[BLOCK * at : BLOCK * (at + 1)])
    return lax.dot_general(rows, stacked, (((1,), (1,)), ((), ())), preferred_element_type=F32)


def lag_sums(total):
    out = []
    for h in range(2):
        for p in range(PAIRS):
            part = total[p * BLOCK : (p + 1) * BLOCK, h * HALF : (h + 1) * HALF]
            part = pltpu.roll(part, HALF - BLOCK + 1, 1, stride=1, stride_axis=0)
            out.append(jnp.sum(part, axis=0, keepdims=True))
    return jnp.concatenate(out, axis=0)


def bands(taps):
    out = []
    for h in range(2):
        groups = []
        for p in range(h * PAIRS, (h + 1) * PAIRS):
            rows = jnp.broadcast_to(taps[p : p + 1], (BLOCK, HALF))
            groups.append(pltpu.roll(rows, 0, 1, stride=1, stride_axis=0))
        out.append(jnp.concatenate(groups, axis=0))
    return jnp.concatenate(out, axis=1)


def backwards_rows(rows):
    i, j = iotas((FILT, FILT))
    flip = (i + j == FILT - 1).astype(BF16)
    return jnp.dot(flip, rows, preferred_element_type=F32).astype(BF16)


def tiled(mask):
    return jnp.concatenate([mask] * PAIRS, axis=0)


def own_kernel(pieces, *refs):
    lens_ref, place_ref = refs[:2]
    mixed_refs = refs[2 : 2 + pieces]
    x_ref, lag_ref, xb_ref, keep_ref, mask_ref, back_ref = refs[2 + pieces :]
    base = place_ref[0] * FILT
    first, count = span(lens_ref, base)
    row, _ = iotas((FILT, TILE))
    keep_ref[0] = (FILT - 1 - row >= first).astype(F32).astype(BF16)
    keep_ref[1] = (row < count).astype(F32).astype(BF16)
    row, _ = iotas((BLOCK, HALF))
    for step in range(STEPS):
        back = own_mask(lens_ref, base, step, True).astype(F32)
        back_ref[step] = jnp.concatenate([back, back], axis=1)
        ahead = own_mask(lens_ref, base, step, False)
        cross = cross_fold(False) & (row + BLOCK * step >= first)
        masks = [mask.astype(F32).astype(BF16) for mask in (ahead, ahead, cross, cross)]
        mask_ref[step] = jnp.concatenate(masks, axis=1)
    tiles = []
    for k in range(pieces):
        for t in range(mixed_refs[k].shape[1] // TILE):
            tiles.append((len(tiles), k, t))
    for at, _, _ in tiles:
        lanes = slice(at * TILE, (at + 1) * TILE)
        xb_ref[:, lanes] = backwards_rows(x_ref[:, lanes])
    for at, k, t in tiles:
        groups = slice(at * 2 * PAIRS, (at + 1) * 2 * PAIRS)
        low, high = halves(mixed_refs[k][:, t * TILE : (t + 1) * TILE])
        x_back = xb_ref[:, at * TILE : (at + 1) * TILE]
        total = None
        for step in range(STEPS):
            stacked = jnp.concatenate([turned(low, step), turned(high, step)], axis=0)
            product = correlate(x_back, step, stacked).reshape(PAIRS, BLOCK, TILE) * back_ref[step][None]
            total = product if total is None else total + product
        lag_ref[groups] = lag_sums(total.reshape(PAIRS * BLOCK, TILE))


def own_part(lens, place, mixed, x):
    channels = x.shape[1]
    pieces = len(mixed)
    return pl.pallas_call(
        functools.partial(own_kernel, pieces),
        in_specs=[SMEM, SMEM] + [VMEM] * (pieces + 1),
        out_specs=[VMEM] * 4,
        out_shape=[
            jax.ShapeDtypeStruct((channels // GROUP, FILT), F32),
            jax.ShapeDtypeStruct((FILT, channels), BF16),
            jax.ShapeDtypeStruct((2, FILT, TILE), BF16),
            jax.ShapeDtypeStruct((STEPS, BLOCK, 2 * TILE), BF16),
        ],
        scratch_shapes=[pltpu.VMEM((STEPS, BLOCK, TILE), F32)],
        compiler_params=pltpu.CompilerParams(vmem_limit_bytes=16 << 20),
        cost_estimate=pl.CostEstimate(flops=2 * FILT * TILE * channels * PAIRS, bytes_accessed=4 << 20, transcendentals=0),
        name="own_part",
    )(lens, place, *mixed, x)


def lag_kernel(first_group, scale, copies, *refs):
    keep_ref, halo_ref, xb_ref, lag_ref = refs[:4]
    out_ref = refs[-1]
    earlier = refs[4:-1]
    fold = cross_fold(True).astype(F32)
    fold = tiled(jnp.concatenate([fold, fold], axis=1))
    if earlier:
        done = earlier[0][...].astype(out_ref.dtype)
        if copies:
            for c in range(copies):
                out_ref[c, :first_group] = done
        else:
            out_ref[:first_group] = done
    for t in range(halo_ref.shape[1] // TILE):
        low, high = halves(halo_ref[:, t * TILE : (t + 1) * TILE] * keep_ref[1])
        at = first_group * GROUP + t * TILE
        x_back = xb_ref[:, at : at + TILE] * keep_ref[0]
        total = None
        for step in range(STEPS):
            stacked = jnp.concatenate([turned_cross(low, step), turned_cross(high, step)], axis=0)
            product = correlate(x_back, step, stacked)
            total = product if total is None else total + product
        rows = first_group + t * 2 * PAIRS
        sums = (lag_ref[rows : rows + 2 * PAIRS] + lag_sums(total * fold)) * scale
        if copies:
            for c in range(copies):
                out_ref[c, rows : rows + 2 * PAIRS] = sums.astype(out_ref.dtype)
        else:
            out_ref[rows : rows + 2 * PAIRS] = sums


def lag_part(keep, halo, x_back, lag, first_group, scale, copies, earlier):
    width = halo.shape[1]
    rows = first_group + width // GROUP
    shape = jax.ShapeDtypeStruct((copies, rows, FILT), SENT) if copies else jax.ShapeDtypeStruct((rows, FILT), F32)
    return pl.pallas_call(
        functools.partial(lag_kernel, first_group, scale, copies),
        in_specs=[VMEM] * (4 + len(earlier)),
        out_specs=VMEM,
        out_shape=shape,
        compiler_params=pltpu.CompilerParams(vmem_limit_bytes=16 << 20),
        cost_estimate=pl.CostEstimate(flops=2 * FILT * TILE * width * PAIRS, bytes_accessed=2 << 20, transcendentals=0),
        name="lag_part",
    )(keep, halo, x_back, lag, *earlier)


def down_kernel(pieces, *refs):
    keep_ref, mask_ref, taps_ref = refs[:3]
    mixed_refs = refs[3 : 3 + pieces]
    halo_refs = refs[3 + pieces : 3 + 2 * pieces]
    out_ref, band_ref, rows_ref, sems = refs[3 + 2 * pieces :]
    tiles = []
    for k in range(pieces):
        for t in range(mixed_refs[k].shape[1] // TILE):
            tiles.append((len(tiles), k, t))
    for at, _, _ in tiles:
        taps = taps_ref[at * 2 * PAIRS : (at + 1) * 2 * PAIRS].astype(BF16).astype(F32)
        band_ref[at * PAIRS * BLOCK : (at + 1) * PAIRS * BLOCK] = bands(taps).astype(BF16)
    copies = []
    for at, k, t in tiles:
        lanes = slice(t * TILE, (t + 1) * TILE)
        low, high = halves(mixed_refs[k][:, lanes])
        next_low, next_high = halves(halo_refs[k][:, lanes] * keep_ref[1])
        band = band_ref[at * PAIRS * BLOCK : (at + 1) * PAIRS * BLOCK]
        band = jnp.concatenate([band, band], axis=1)
        for step in range(STEPS):
            stacked = [turned(low, step), turned(high, step), turned_cross(next_low, step), turned_cross(next_high, step)]
            stacked = jnp.concatenate(stacked, axis=0)
            product = jnp.dot(band * tiled(mask_ref[step]), stacked, preferred_element_type=F32)
            rows_ref[BLOCK * step : BLOCK * (step + 1), at * TILE : (at + 1) * TILE] = pick_groups(product).astype(BF16)
        lanes = slice(at * TILE, (at + 1) * TILE)
        copy = pltpu.make_async_copy(rows_ref.at[:, lanes], out_ref.at[:, lanes], sems.at[at])
        copy.start()
        copies.append(copy)
    for copy in copies:
        copy.wait()


def down_part(keep, masks, taps, mixed, halos):
    pieces = len(mixed)
    channels = taps.shape[0] * GROUP
    tiles = channels // TILE
    return pl.pallas_call(
        functools.partial(down_kernel, pieces),
        in_specs=[VMEM] * (3 + 2 * pieces),
        out_specs=pl.BlockSpec(memory_space=pl.ANY),
        out_shape=jax.ShapeDtypeStruct((FILT, channels), BF16),
        scratch_shapes=[
            pltpu.VMEM((tiles * PAIRS * BLOCK, TILE), BF16),
            pltpu.VMEM((FILT, channels), BF16),
            pltpu.SemaphoreType.DMA((tiles,)),
        ],
        compiler_params=pltpu.CompilerParams(vmem_limit_bytes=16 << 20),
        cost_estimate=pl.CostEstimate(flops=4 * FILT * TILE * channels * PAIRS, bytes_accessed=4 << 20, transcendentals=0),
        name="down_part",
    )(keep, masks, taps, *mixed, *halos)


def shards(gate_branch, conv_input, grad_output, filter_taps, document_lengths):
    local_rows, channels = gate_branch.shape
    ctx_count = lax.axis_size("ctx")
    dp_count = lax.axis_size("dp")
    grad_scale = (1.0 * GROUP * dp_count * local_rows * ctx_count) ** (-0.5)
    place = lax.axis_index("ctx").astype(jnp.int32).reshape(1)
    cuts = [0, channels * 3 // 4, channels * 7 // 8, channels]
    back = [(i, i - 1) for i in range(1, ctx_count)]
    mixed, halos = [], []
    gate, grad = gate_branch, grad_output
    for low, high in zip(cuts, cuts[1:]):
        if len(mixed) == 1:
            gate, grad, mixed[-1] = lax.optimization_barrier((gate, grad, mixed[-1]))
        mixed.append((grad[:, low:high].astype(F32) * gate[:, low:high].astype(F32)).astype(BF16))
        halos.append(lax.ppermute(mixed[-1], "ctx", back))
    pieces = len(mixed)
    lag, x_back, keep, masks = own_part(document_lengths, place, mixed, conv_input)
    sums = []
    for k in range(pieces):
        copies = dp_count if k == pieces - 1 else 0
        sums = [lag_part(keep, halos[k], x_back, lag, cuts[k] // GROUP, grad_scale, copies, sums)]
    partial = sums[0].reshape(dp_count * ctx_count, -1, FILT)
    shared = lax.all_to_all(partial, ("dp", "ctx"), 0, 0, tiled=True)
    filter_grad = jnp.sum(shared.astype(F32), axis=0)
    grad_input = down_part(keep, masks, filter_taps, mixed, halos)
    return grad_input, filter_grad


def solution(mesh):
    rows = P(("dp", "ctx"), None)
    return jax.shard_map(
        shards,
        mesh=mesh,
        in_specs=(rows, rows, rows, P(), P("dp", None)),
        out_specs=(rows, P("ctx", None)),
        check_vma=False,
    )
```

```python
import functools

import jax
import jax.numpy as jnp
from jax import lax
from jax.experimental import pallas as pl
from jax.experimental.pallas import tpu as pltpu
from jax.sharding import PartitionSpec as P

GROUP = 16
FILT = 128
TILE = 256
HALF = 128
PAIRS = HALF // GROUP
BLOCK = 32
STEPS = FILT // BLOCK
BIG = 1 << 30
F32 = jnp.float32
BF16 = jnp.bfloat16
SENT = jnp.bfloat16
VMEM = pl.BlockSpec(memory_space=pltpu.VMEM)
SMEM = pl.BlockSpec(memory_space=pltpu.SMEM)


def iotas(shape):
    return lax.broadcasted_iota(jnp.int32, shape, 0), lax.broadcasted_iota(jnp.int32, shape, 1)


def own_mask(lens_ref, base, step, backwards):
    b, k = iotas((BLOCK, HALF))
    if backwards:
        b = BLOCK - 1 - b
    row = b + BLOCK * step
    limit = jnp.full((BLOCK, HALF), FILT, jnp.int32)
    end = -base
    for n in range(lens_ref.shape[1]):
        end = end + lens_ref[0, n]
        limit = jnp.minimum(limit, jnp.where(row < end, end, BIG))
    return row + ((k - b) & (FILT - 1)) < limit


def span(lens_ref, base):
    first, count = jnp.int32(-BIG), jnp.int32(BIG)
    end = -base
    for n in range(lens_ref.shape[1]):
        end = end + lens_ref[0, n]
        inside = end < FILT
        first = jnp.where(inside, end, first)
        count = jnp.where(inside, count, jnp.minimum(count, end - FILT))
    return first, count


def cross_fold(backwards):
    b, k = iotas((BLOCK, HALF))
    if backwards:
        b = BLOCK - 1 - b
    return (k >= BLOCK) | (k < b)


def halves(rows):
    lane = lax.broadcasted_iota(jnp.int32, rows.shape, 1)
    zero = jnp.zeros_like(rows)
    return jnp.where(lane < HALF, rows, zero), jnp.where(lane >= HALF, rows, zero)


def turned(rows, step):
    if step == 0:
        return rows
    return jnp.concatenate([rows[BLOCK * step :], rows[: BLOCK * step]], axis=0)


def turned_cross(rows, step):
    parts = [rows[BLOCK * step : BLOCK * (step + 1)]]
    if step < STEPS - 1:
        parts.append(jnp.zeros((BLOCK * (STEPS - 1 - step), rows.shape[1]), rows.dtype))
    if step > 0:
        parts.append(rows[: BLOCK * step])
    return jnp.concatenate(parts, axis=0)


def split_groups(rows):
    which = (lax.broadcasted_iota(jnp.int32, rows.shape, 1) % HALF) // GROUP
    zero = jnp.zeros_like(rows)
    return jnp.concatenate([jnp.where(which == p, rows, zero) for p in range(PAIRS)], axis=0)


def pick_groups(stacked):
    which = (lax.broadcasted_iota(jnp.int32, (BLOCK, TILE), 1) % HALF) // GROUP
    out = stacked[:BLOCK]
    for p in range(1, PAIRS):
        out = jnp.where(which == p, stacked[p * BLOCK : (p + 1) * BLOCK], out)
    return out


def correlate(x_back, step, stacked):
    at = STEPS - 1 - step
    rows = split_groups(x_back[BLOCK * at : BLOCK * (at + 1)])
    return lax.dot_general(rows, stacked, (((1,), (1,)), ((), ())), preferred_element_type=F32)


def lag_sums(total):
    out = []
    for h in range(2):
        for p in range(PAIRS):
            part = total[p * BLOCK : (p + 1) * BLOCK, h * HALF : (h + 1) * HALF]
            part = pltpu.roll(part, HALF - BLOCK + 1, 1, stride=1, stride_axis=0)
            out.append(jnp.sum(part, axis=0, keepdims=True))
    return jnp.concatenate(out, axis=0)


def bands(taps):
    out = []
    for h in range(2):
        groups = []
        for p in range(h * PAIRS, (h + 1) * PAIRS):
            rows = jnp.broadcast_to(taps[p : p + 1], (BLOCK, HALF))
            groups.append(pltpu.roll(rows, 0, 1, stride=1, stride_axis=0))
        out.append(jnp.concatenate(groups, axis=0))
    return jnp.concatenate(out, axis=1)


def backwards_rows(rows):
    i, j = iotas((FILT, FILT))
    flip = (i + j == FILT - 1).astype(BF16)
    return jnp.dot(flip, rows, preferred_element_type=F32).astype(BF16)


def tiled(mask):
    return jnp.concatenate([mask] * PAIRS, axis=0)


def own_kernel(pieces, *refs):
    lens_ref, place_ref = refs[:2]
    mixed_refs = refs[2 : 2 + pieces]
    x_ref, lag_ref, xb_ref, keep_ref, mask_ref, back_ref = refs[2 + pieces :]
    base = place_ref[0] * FILT
    first, count = span(lens_ref, base)
    row, _ = iotas((FILT, TILE))
    keep_ref[0] = (FILT - 1 - row >= first).astype(F32).astype(BF16)
    keep_ref[1] = (row < count).astype(F32).astype(BF16)
    row, _ = iotas((BLOCK, HALF))
    for step in range(STEPS):
        back = own_mask(lens_ref, base, step, True).astype(F32)
        back_ref[step] = jnp.concatenate([back, back], axis=1)
        ahead = own_mask(lens_ref, base, step, False)
        cross = cross_fold(False) & (row + BLOCK * step >= first)
        masks = [mask.astype(F32).astype(BF16) for mask in (ahead, ahead, cross, cross)]
        mask_ref[step] = jnp.concatenate(masks, axis=1)
    tiles = []
    for k in range(pieces):
        for t in range(mixed_refs[k].shape[1] // TILE):
            tiles.append((len(tiles), k, t))
    for at, _, _ in tiles:
        lanes = slice(at * TILE, (at + 1) * TILE)
        xb_ref[:, lanes] = backwards_rows(x_ref[:, lanes])
    for at, k, t in tiles:
        groups = slice(at * 2 * PAIRS, (at + 1) * 2 * PAIRS)
        low, high = halves(mixed_refs[k][:, t * TILE : (t + 1) * TILE])
        x_back = xb_ref[:, at * TILE : (at + 1) * TILE]
        total = None
        for step in range(STEPS):
            stacked = jnp.concatenate([turned(low, step), turned(high, step)], axis=0)
            product = correlate(x_back, step, stacked).reshape(PAIRS, BLOCK, TILE) * back_ref[step][None]
            total = product if total is None else total + product
        lag_ref[groups] = lag_sums(total.reshape(PAIRS * BLOCK, TILE))
        xb_ref[:, at * TILE : (at + 1) * TILE] = x_back * keep_ref[0]


def own_part(lens, place, mixed, x):
    channels = x.shape[1]
    pieces = len(mixed)
    return pl.pallas_call(
        functools.partial(own_kernel, pieces),
        in_specs=[SMEM, SMEM] + [VMEM] * (pieces + 1),
        out_specs=[VMEM] * 4,
        out_shape=[
            jax.ShapeDtypeStruct((channels // GROUP, FILT), F32),
            jax.ShapeDtypeStruct((FILT, channels), BF16),
            jax.ShapeDtypeStruct((2, FILT, TILE), BF16),
            jax.ShapeDtypeStruct((STEPS, BLOCK, 2 * TILE), BF16),
        ],
        scratch_shapes=[pltpu.VMEM((STEPS, BLOCK, TILE), F32)],
        compiler_params=pltpu.CompilerParams(vmem_limit_bytes=16 << 20),
        cost_estimate=pl.CostEstimate(flops=2 * FILT * TILE * channels * PAIRS, bytes_accessed=4 << 20, transcendentals=0),
        name="own_part",
    )(lens, place, *mixed, x)


def lag_kernel(first_group, scale, copies, *refs):
    keep_ref, halo_ref, xb_ref, lag_ref = refs[:4]
    out_ref = refs[-1]
    earlier = refs[4:-1]
    fold = cross_fold(True).astype(F32)
    fold = tiled(jnp.concatenate([fold, fold], axis=1))
    if earlier:
        done = earlier[0][...].astype(out_ref.dtype)
        if copies:
            for c in range(copies):
                out_ref[c, :first_group] = done
        else:
            out_ref[:first_group] = done
    for t in range(halo_ref.shape[1] // TILE):
        low, high = halves(halo_ref[:, t * TILE : (t + 1) * TILE] * keep_ref[1])
        at = first_group * GROUP + t * TILE
        x_back = xb_ref[:, at : at + TILE]
        total = None
        for step in range(STEPS):
            stacked = jnp.concatenate([turned_cross(low, step), turned_cross(high, step)], axis=0)
            product = correlate(x_back, step, stacked)
            total = product if total is None else total + product
        rows = first_group + t * 2 * PAIRS
        sums = (lag_ref[rows : rows + 2 * PAIRS] + lag_sums(total * fold)) * scale
        if copies:
            for c in range(copies):
                out_ref[c, rows : rows + 2 * PAIRS] = sums.astype(out_ref.dtype)
        else:
            out_ref[rows : rows + 2 * PAIRS] = sums


def lag_part(keep, halo, x_back, lag, first_group, scale, copies, earlier):
    width = halo.shape[1]
    rows = first_group + width // GROUP
    shape = jax.ShapeDtypeStruct((copies, rows, FILT), SENT) if copies else jax.ShapeDtypeStruct((rows, FILT), F32)
    return pl.pallas_call(
        functools.partial(lag_kernel, first_group, scale, copies),
        in_specs=[VMEM] * (4 + len(earlier)),
        out_specs=VMEM,
        out_shape=shape,
        compiler_params=pltpu.CompilerParams(vmem_limit_bytes=16 << 20),
        cost_estimate=pl.CostEstimate(flops=2 * FILT * TILE * width * PAIRS, bytes_accessed=2 << 20, transcendentals=0),
        name="lag_part",
    )(keep, halo, x_back, lag, *earlier)


def down_kernel(pieces, *refs):
    keep_ref, mask_ref, taps_ref = refs[:3]
    mixed_refs = refs[3 : 3 + pieces]
    halo_refs = refs[3 + pieces : 3 + 2 * pieces]
    out_ref, band_ref, rows_ref, sems = refs[3 + 2 * pieces :]
    tiles = []
    for k in range(pieces):
        for t in range(mixed_refs[k].shape[1] // TILE):
            tiles.append((len(tiles), k, t))
    for at, _, _ in tiles:
        taps = taps_ref[at * 2 * PAIRS : (at + 1) * 2 * PAIRS].astype(BF16).astype(F32)
        band_ref[at * PAIRS * BLOCK : (at + 1) * PAIRS * BLOCK] = bands(taps).astype(BF16)
    copies = []
    for at, k, t in tiles:
        lanes = slice(t * TILE, (t + 1) * TILE)
        low, high = halves(mixed_refs[k][:, lanes])
        next_low, next_high = halves(halo_refs[k][:, lanes] * keep_ref[1])
        band = band_ref[at * PAIRS * BLOCK : (at + 1) * PAIRS * BLOCK]
        band = jnp.concatenate([band, band], axis=1)
        for step in range(STEPS):
            stacked = [turned(low, step), turned(high, step), turned_cross(next_low, step), turned_cross(next_high, step)]
            stacked = jnp.concatenate(stacked, axis=0)
            product = jnp.dot(band * tiled(mask_ref[step]), stacked, preferred_element_type=F32)
            rows_ref[BLOCK * step : BLOCK * (step + 1), at * TILE : (at + 1) * TILE] = pick_groups(product).astype(BF16)
        lanes = slice(at * TILE, (at + 1) * TILE)
        copy = pltpu.make_async_copy(rows_ref.at[:, lanes], out_ref.at[:, lanes], sems.at[at])
        copy.start()
        copies.append(copy)
    for copy in copies:
        copy.wait()


def down_part(keep, masks, taps, mixed, halos):
    pieces = len(mixed)
    channels = taps.shape[0] * GROUP
    tiles = channels // TILE
    return pl.pallas_call(
        functools.partial(down_kernel, pieces),
        in_specs=[VMEM] * (3 + 2 * pieces),
        out_specs=pl.BlockSpec(memory_space=pl.ANY),
        out_shape=jax.ShapeDtypeStruct((FILT, channels), BF16),
        scratch_shapes=[
            pltpu.VMEM((tiles * PAIRS * BLOCK, TILE), BF16),
            pltpu.VMEM((FILT, channels), BF16),
            pltpu.SemaphoreType.DMA((tiles,)),
        ],
        compiler_params=pltpu.CompilerParams(vmem_limit_bytes=16 << 20),
        cost_estimate=pl.CostEstimate(flops=4 * FILT * TILE * channels * PAIRS, bytes_accessed=4 << 20, transcendentals=0),
        name="down_part",
    )(keep, masks, taps, *mixed, *halos)


def shards(gate_branch, conv_input, grad_output, filter_taps, document_lengths):
    local_rows, channels = gate_branch.shape
    ctx_count = lax.axis_size("ctx")
    dp_count = lax.axis_size("dp")
    grad_scale = (1.0 * GROUP * dp_count * local_rows * ctx_count) ** (-0.5)
    place = lax.axis_index("ctx").astype(jnp.int32).reshape(1)
    cuts = [0, channels * 5 // 8, channels * 13 // 16, channels]
    back = [(i, i - 1) for i in range(1, ctx_count)]
    mixed, halos = [], []
    gate, grad = gate_branch, grad_output
    for low, high in zip(cuts, cuts[1:]):
        if len(mixed) == 1:
            gate, grad, mixed[-1] = lax.optimization_barrier((gate, grad, mixed[-1]))
        mixed.append((grad[:, low:high].astype(F32) * gate[:, low:high].astype(F32)).astype(BF16))
        halos.append(lax.ppermute(mixed[-1], "ctx", back))
    pieces = len(mixed)
    lag, x_back, keep, masks = own_part(document_lengths, place, mixed, conv_input)
    sums = []
    for k in range(pieces):
        copies = dp_count if k == pieces - 1 else 0
        sums = [lag_part(keep, halos[k], x_back, lag, cuts[k] // GROUP, grad_scale, copies, sums)]
    partial = sums[0].reshape(dp_count * ctx_count, -1, FILT)
    shared = lax.all_to_all(partial, ("dp", "ctx"), 0, 0, tiled=True)
    filter_grad = jnp.sum(shared.astype(F32), axis=0)
    grad_input = down_part(keep, masks, filter_taps, mixed, halos)
    return grad_input, filter_grad


def solution(mesh):
    rows = P(("dp", "ctx"), None)
    return jax.shard_map(
        shards,
        mesh=mesh,
        in_specs=(rows, rows, rows, P(), P("dp", None)),
        out_specs=(rows, P("ctx", None)),
        check_vma=False,
    )
```
